512 devices in a mesh: seq: 64 (over x, z), head: 8 (over y, core).
Axes of the slice: x: 4, y: 4, z: 16, core: 2. Of those that a mesh axis runs over, the one named last changes fastest.
Arguments:
- queries: bfloat16 [32768, 1024], P('seq', 'head'), may hold values from -13 to 13
- keys: bfloat16 [32768, 128], P(('seq', 'head')), may hold values from -4.5 to 4.5
- values: bfloat16 [32768, 128], P(('seq', 'head')), may hold values from -6 to 6
- req_lengths: int32 [16], replicated, may hold values from 1 to 128, 256 in all
Outputs:
- attended: bfloat16 [32768, 1024], P('seq', 'head')
The draws below stay inside these ranges and needn't reach their ends.
Inputs may be any that keep to these rules, and one draw needn't show every extreme that they name: `req_lengths`: requests cover all 32768 tokens end to end; the longest has exactly 16384 tokens.
All inputs are finite; a program needn't handle non-finite values.
Results may differ from the reference program's by a relative error of at most 0.0045.
Values may be sent and summed in bfloat16 or wider, within the bound.
A program may use at most 64 MiB of HBM per device.

```python
import math
import jax
import jax.numpy as jnp
import numpy as np
from jax import lax

HD = 128
HEADS = 8
TOK_DEV = 512
SPAN = 32
TOKENS = 32768
PAGE = 128
MOST = 16384
REQS = 16
N_SEQ = 64


def draw_queries(key, part):
    key = jax.random.fold_in(key, 7)
    drawn = 1.5 * jax.random.truncated_normal(key, -6.0, 6.0, (TOKENS, HEADS * HD), jnp.float32)
    return drawn.astype(jnp.bfloat16)


def draw_keys(key, part):
    key = jax.random.fold_in(key, 11)
    drawn = jax.random.truncated_normal(key, -4.5, 4.5, (TOKENS, HD), jnp.float32)
    return drawn.astype(jnp.bfloat16)


def steps_of(key, dims, shards, least, top_value):
    gain = 1.0
    for position, parts in shards:
        steps = jax.random.uniform(jax.random.fold_in(jax.random.fold_in(key, 6), position), (parts,), jnp.float32, least / len(shards), top_value / len(shards))
        gain = gain * jnp.repeat(jnp.exp(steps), dims[position] // parts).reshape((-1,) + (1,) * (len(dims) - 1 - position))
    return gain


def profile(count, total, bound, lean):
    weights = [(1 << 20) // math.isqrt(standing ** lean) + 1 for standing in range(2, count + 1)]
    surplus, counts = total - bound - (count - 1), [1] * (count - 1)
    while surplus > 0:
        candidates = [i for i in range(count - 1) if counts[i] < bound]
        pool, budget = sum([weights[i] for i in candidates]), surplus
        for i in candidates:
            addition = min(bound - counts[i], max(1, budget * weights[i] // pool), surplus)
            counts[i] = counts[i] + addition
            surplus = surplus - addition
    return np.array([bound] + counts)


def ragged_sizes(stream_key, amount, total, bound, skew):
    if amount == 2:
        one = jax.random.randint(stream_key, (), max(1, total - bound), min(bound, total - 1) + 1)
        return jnp.stack([one, total - one])
    sizes = jnp.asarray(profile(amount, total, bound, skew), jnp.int32)
    couples = (amount - 1) // 2
    source_of, receiver = sizes[1:1 + 2 * couples:2], sizes[2:2 + 2 * couples:2]
    room = jnp.minimum(source_of - 1, bound - receiver)
    passed = jax.random.randint(jax.random.fold_in(stream_key, 1), (couples,), 0, 1 << 20) % (room + 1)
    sizes = sizes.at[1:1 + 2 * couples:2].set(source_of - passed).at[2:2 + 2 * couples:2].set(receiver + passed)
    return sizes[jax.random.permutation(jax.random.fold_in(stream_key, 2), amount)]


def gaussian(rng, dims, scale, limit, cuts=(), held_as=jnp.bfloat16):
    gain = steps_of(rng, dims, cuts, -0.22, 0.18) if cuts else 1.0
    values = jax.random.normal(rng, dims, jnp.float32) * scale * gain
    return jnp.minimum(jnp.maximum(values, -limit), limit).astype(held_as)


def setup_inputs(seed: int = 0) -> dict:
    seeds = jax.random.split(jax.random.key(seed), 5)
    queries = draw_queries(jax.random.fold_in(seeds[4], 71), 0)
    keys = draw_keys(jax.random.fold_in(seeds[4], 71), 0)
    values = gaussian(seeds[2], (TOKENS, HD), 1.0, 6.0, ((0, 512),))
    req_lengths = ragged_sizes(seeds[3], REQS, TOKENS // PAGE, MOST // PAGE, 2).astype(jnp.int32)
    return dict(queries=queries, keys=keys, values=values, req_lengths=req_lengths)


def token_starts(req_lengths, first_token, row_count):
    lengths = req_lengths.astype(jnp.int32) * PAGE
    request_ends = jnp.cumsum(lengths).astype(jnp.int32)
    request_starts = (request_ends - lengths).astype(jnp.int32)
    positions = first_token + jnp.arange(row_count, dtype=jnp.int32)
    inside = request_starts[None, :] <= positions[:, None]
    return lax.optimization_barrier(jnp.max(jnp.where(inside, request_starts[None, :], 0), axis=1)).astype(jnp.int32)

def reference(queries, keys, values, req_lengths):
    score_scale = 1.0 / math.sqrt(HD)
    window_rows = (SPAN + 1) * TOK_DEV

    def one_block(block_index):
        first_token = (block_index * TOK_DEV).astype(jnp.int32)
        lowest_key = (jnp.maximum(block_index - SPAN, 0) * TOK_DEV).astype(jnp.int32)
        query_rows = lax.dynamic_slice_in_dim(queries, first_token, TOK_DEV, 0)
        query_rows = query_rows.astype(jnp.float32).reshape(TOK_DEV, HEADS, HD)
        key_rows = lax.dynamic_slice_in_dim(keys, lowest_key, window_rows, 0).astype(jnp.float32)
        value_rows = lax.dynamic_slice_in_dim(values, lowest_key, window_rows, 0).astype(jnp.float32)
        scores = jnp.einsum('qhd,kd->hqk', query_rows, key_rows) * score_scale
        query_pos = first_token + jnp.arange(TOK_DEV, dtype=jnp.int32)
        key_pos = lowest_key + jnp.arange(window_rows, dtype=jnp.int32)
        query_start = token_starts(req_lengths, first_token, TOK_DEV)
        visible = (key_pos[None, :] >= query_start[:, None]) & (key_pos[None, :] <= query_pos[:, None])
        masked = jnp.where(visible[None], scores, -jnp.inf)
        row_max = lax.optimization_barrier(jnp.max(masked, axis=2, keepdims=True))
        exp_terms = jnp.where(visible[None], jnp.exp(scores - row_max), 0.0)
        totals = lax.optimization_barrier(jnp.sum(exp_terms, axis=2))
        weights = lax.optimization_barrier(exp_terms.astype(jnp.bfloat16))
        weighted = jnp.einsum('hqk,kd->qhd', weights.astype(jnp.float32), value_rows)
        output = weighted / jnp.transpose(totals)[:, :, None]
        return output.reshape(TOK_DEV, HEADS * HD).astype(jnp.bfloat16)
    per_block = lax.map(one_block, jnp.arange(N_SEQ, dtype=jnp.int32))
    return per_block.reshape(TOKENS, HEADS * HD)
```

```python
import functools
import math

import jax
import jax.numpy as jnp
from jax import lax
from jax.experimental import pallas as pl
from jax.experimental.pallas import tpu as pltpu
from jax.sharding import PartitionSpec as P

HD = 128
PAGE = 128
NX, NY, NZ = 4, 4, 16
REQS = 16
SCALE = math.log2(math.e) / math.sqrt(HD)
LOW = -1e15
BIG = 1e30
NT = (((1,), (1,)), ((), ()))
NN = (((1,), (0,)), ((), ()))
MESH = pl.DeviceIdType.MESH
HALFWAY = NZ // 2


def dot(a, b, dims):
    return lax.dot_general(a, b, dims, preferred_element_type=jnp.float32)


def kernel(q_ref, k_ref, v_ref, len_ref, o_ref,
           qbuf, raw, kv, acc, mrow, starts, obuf, lbuf, osend, lsend,
           q_ss, q_rs, i_ss, i_rs, z_ss, z_rs, x_ss, x_rs, d_ss, d_rs, o_ss, o_rs, l_ss, l_rs):
    rows = q_ref.shape[0]
    seq = lax.axis_index("seq")
    head = lax.axis_index("head")
    x, z = seq // NZ, seq % NZ
    y, c = head // 2, head % 2
    way = 1 - 2 * c

    def at(dx, dy, dz, core):
        xx = (x + dx + NX) % NX
        yy = (y + dy) % NY
        zz = (z + dz + NZ) % NZ
        return (xx * NZ + zz, yy * 2 + core)

    barrier = pltpu.get_barrier_semaphore()
    partners = [at(0, 0, 0, 1 - c), at(0, 0, 1, c), at(0, 0, -1, c)]
    partners += [at(dx, 0, 0, core) for dx in (1, -1, 2) for core in (c, 1 - c)]
    partners += [at(0, dy, 0, c) for dy in (1, 2, 3)]
    for partner in partners:
        pl.semaphore_signal(barrier, inc=1, device_id=partner, device_id_type=MESH)

    raw[0, c, 0] = k_ref[...]
    raw[0, c, 1] = v_ref[...]
    qbuf[0] = q_ref[...]
    acc[...] = jnp.zeros_like(acc)
    mrow[...] = jnp.full_like(mrow, LOW)
    row_page = seq * (rows // PAGE) + lax.broadcasted_iota(jnp.int32, (1, rows), 1) // PAGE
    start = jnp.int32(0)
    found = jnp.zeros((1, rows), jnp.int32)
    for r in range(REQS):
        found = jnp.maximum(found, jnp.where(row_page >= start, start, 0))
        start = start + len_ref[r]
    starts[...] = found

    pl.semaphore_wait(barrier, len(partners))

    def remote(src, dst, ssem, rsem, to):
        return pltpu.make_async_remote_copy(
            src_ref=src, dst_ref=dst, send_sem=ssem, recv_sem=rsem, device_id=to, device_id_type=MESH)

    def init_copy(n):
        dx, core = ((0, 1 - c), (1, c), (1, 1 - c), (2, c), (2, 1 - c))[n]
        return remote(raw.at[0, c], raw.at[dx, c], i_ss.at[n], i_rs.at[n], at(dx, 0, 0, core))

    def init_wait(n):
        dx, core = ((0, 1 - c), (1, c), (1, 1 - c), (2, c), (2, 1 - c))[n]
        remote(raw.at[dx, core], raw.at[dx, core], i_ss.at[n], i_rs.at[n], at(0, 0, 0, 1 - c)).wait_recv()

    def q_copy(j):
        return remote(qbuf.at[0], qbuf.at[j], q_ss.at[j], q_rs.at[j], at(0, NY - j, 0, c))

    def zpos(t):
        return (z - way * t + 2 * NZ) % NZ

    def zother(t):
        return (z + way * t + 2 * NZ) % NZ

    def slot(dx, zz):
        return dx * NZ + zz

    def far(zz):
        return jnp.where(zz < z, 0, 2)

    def z_copy(part, t):
        s = slot(2 * part, zpos(t - 1))
        return remote(kv.at[s], kv.at[s], z_ss.at[part, t], z_rs.at[part, t], at(0, 0, way, c))

    def z_wait(part, t):
        s = slot(2 * part, zpos(t))
        remote(kv.at[s], kv.at[s], z_ss.at[part, t], z_rs.at[part, t], at(0, 0, way, c)).wait_recv()

    def x_copy(t):
        zz = zpos(t)
        return remote(kv.at[slot(0, zz)], kv.at[slot(1, zz)], x_ss.at[t], x_rs.at[t], at(1, 0, 0, c))

    def x_wait(t):
        s = slot(1, zpos(t))
        remote(kv.at[s], kv.at[s], x_ss.at[t], x_rs.at[t], at(1, 0, 0, c)).wait_recv()

    def d_slot(part, zz):
        return slot(1, zz) if part else slot(far(zz), zz)

    def d_copy(part, t):
        s = d_slot(part, zpos(t))
        return remote(kv.at[s], kv.at[s], d_ss.at[part, t], d_rs.at[part, t], at(0, 0, 0, 1 - c))

    def d_wait(part, t):
        s = d_slot(part, zother(t))
        remote(kv.at[s], kv.at[s], d_ss.at[part, t], d_rs.at[part, t], at(0, 0, 0, 1 - c)).wait_recv()

    def assemble(dx):
        s = slot(dx, z)
        kv[s, 0] = jnp.concatenate([raw[dx, 0, 0], raw[dx, 1, 0]], axis=0)
        values = jnp.concatenate([raw[dx, 0, 1], raw[dx, 1, 1]], axis=0)
        kv[s, 1] = values.T

    def ring(t):
        z_wait(0, t)

        @pl.when((t < HALFWAY - 1) | ((t < HALFWAY) & (c == 0)))
        def _():
            z_copy(0, t + 1).start()
        x_copy(t).start()
        z_wait(1, t)

        @pl.when((t < HALFWAY - 1) | ((t < HALFWAY) & (c == 0)))
        def _():
            z_copy(1, t + 1).start()
        d_copy(0, t).start()

    def across(t):
        x_wait(t)
        d_copy(1, t).start()

    def page_of(dx, zz):
        return ((x - dx) * NZ + zz) * (rows // PAGE) + y

    def chunk(pages, heads, diagonal=None, after=None):
        slots = [slot(dx, zz) for dx, zz in pages]
        ks = jnp.concatenate([kv[s, 0] for s in slots], axis=0)
        vt = jnp.concatenate([kv[s, 1] for s in slots], axis=1)
        vt = jnp.concatenate([vt, jnp.ones((16, vt.shape[1]), jnp.bfloat16)], axis=0)
        first = starts[...]
        bias = [jnp.where(first <= page_of(dx, zz), 0.0, -BIG) for dx, zz in pages]
        if diagonal is not None:
            key = y * PAGE + lax.broadcasted_iota(jnp.int32, (PAGE, rows), 0)
            row = lax.broadcasted_iota(jnp.int32, (PAGE, rows), 1)
            causal = key <= row
        scores = [dot(ks, qbuf[h], NT) for h in heads]
        for h, st in zip(heads, scores):
            old = mrow[h]
            new = old
            parts = []
            for n in range(len(pages)):
                part = st[n * PAGE:(n + 1) * PAGE] * SCALE
                if n == diagonal:
                    part = jnp.where(causal, part, -BIG)
                parts.append(part)
                new = jnp.maximum(new, jnp.max(part, axis=0, keepdims=True) + bias[n])
            terms = [jnp.exp2(parts[n] - (new - bias[n])) for n in range(len(pages))]
            factor = jnp.exp2(old - new)
            mrow[h] = new
            update = dot(vt, jnp.concatenate(terms, axis=0).astype(jnp.bfloat16), NN)
            acc[h] = acc[h] * factor + update
            if after is not None:
                after(h)

    def finish(h):
        total = jnp.maximum(acc[h, HD:HD + 1, :], 1e-30)
        part = acc[h, :HD, :] / total
        level = mrow[h] + jnp.log2(total)
        return part, level

    def o_copy(j):
        return remote(osend.at[j - 1], obuf.at[j - 1], o_ss.at[j], o_rs.at[j], at(0, j, 0, c))

    def l_copy(j):
        return remote(lsend.at[j - 1], lbuf.at[j - 1], l_ss.at[j], l_rs.at[j], at(0, j, 0, c))

    def give(h):
        if h > 0:
            part, level = finish(h)
            osend[h - 1] = part.astype(jnp.bfloat16)
            lsend[h - 1] = jnp.broadcast_to(level, lsend.shape[1:])
            o_copy(h).start()
            l_copy(h).start()

    for n in range(5):
        init_copy(n).start()
    for j in (1, 3, 2):
        q_copy(j).start()

    init_wait(0)
    assemble(0)
    z_copy(0, 1).start()
    init_wait(3)
    init_wait(4)
    assemble(2)
    z_copy(1, 1).start()
    init_wait(1)
    init_wait(2)
    assemble(1)
    own = [(0, z), (1, z), (2, z)]
    chunk(own, [0], 0)
    ring(1)
    for j in (1, 3):
        q_copy(j).wait_recv()
    chunk(own, [1, 3], 0)
    ring(2)
    across(1)
    q_copy(2).wait_recv()
    chunk(own, [2], 0)
    d_wait(0, 1)
    everyone = [2, 1, 3, 0]
    chunk([(far(zpos(1)), zpos(1)), (far(zother(1)), zother(1))], everyone)

    def turn(t, _):
        @pl.when((t < HALFWAY) | (c == 0))
        def _():
            ring(t)
        across(t - 1)
        d_wait(0, t - 1)
        d_wait(1, t - 2)
        chunk([(far(zpos(t - 1)), zpos(t - 1)), (far(zother(t - 1)), zother(t - 1)),
               (1, zpos(t - 2)), (1, zother(t - 2))], everyone)
        return 0

    lax.fori_loop(3, HALFWAY + 1, turn, 0)

    @pl.when(c == 0)
    def _():
        across(HALFWAY)

    @pl.when(c == 1)
    def _():
        d_wait(0, HALFWAY)
        d_wait(1, HALFWAY)
    d_wait(1, HALFWAY - 1)
    opposite = zpos(HALFWAY)
    chunk([(far(opposite), opposite), (1, zpos(HALFWAY - 1)), (1, zother(HALFWAY - 1)), (1, opposite)],
          everyone, after=give)

    part, level = finish(0)
    for j in (1, 2, 3):
        o_copy(j).wait_recv()
        l_copy(j).wait_recv()
    levels = [level] + [lbuf[j, 0:1, :] for j in range(3)]
    top = functools.reduce(jnp.maximum, levels)
    shares = [jnp.exp2(level - top) for level in levels]
    total = functools.reduce(jnp.add, shares)
    mixed = part * (shares[0] / total)
    for j in range(3):
        mixed = mixed + obuf[j].astype(jnp.float32) * (shares[j + 1] / total)
    o_ref[...] = mixed.T.astype(o_ref.dtype)

    for n in range(5):
        init_copy(n).wait_send()
    for j in (1, 2, 3):
        q_copy(j).wait_send()
        o_copy(j).wait_send()
        l_copy(j).wait_send()

    def drain(t, _):
        for part in (0, 1):
            z_copy(part, t).wait_send()
            d_copy(part, t).wait_send()
        x_copy(t).wait_send()
        return 0

    lax.fori_loop(1, HALFWAY, drain, 0)

    @pl.when(c == 0)
    def _():
        drain(HALFWAY, 0)


def body(queries, keys, values, req_lengths):
    rows = queries.shape[0]
    bf, f32, dma = jnp.bfloat16, jnp.float32, pltpu.SemaphoreType.DMA
    n = HALFWAY + 1
    return pl.pallas_call(
        kernel,
        out_shape=jax.ShapeDtypeStruct((rows, HD), bf),
        in_specs=[pl.BlockSpec(memory_space=pltpu.VMEM)] * 3 + [pl.BlockSpec(memory_space=pltpu.SMEM)],
        out_specs=pl.BlockSpec(memory_space=pltpu.VMEM),
        scratch_shapes=[
            pltpu.VMEM((NY, rows, HD), bf),
            pltpu.VMEM((3, 2, 2, PAGE // 2, HD), bf),
            pltpu.VMEM((3 * NZ, 2, PAGE, HD), bf),
            pltpu.VMEM((NY, HD + 16, rows), f32),
            pltpu.VMEM((NY, 1, rows), f32),
            pltpu.VMEM((1, rows), jnp.int32),
            pltpu.VMEM((NY - 1, HD, rows), bf),
            pltpu.VMEM((NY - 1, 8, rows), f32),
            pltpu.VMEM((NY - 1, HD, rows), bf),
            pltpu.VMEM((NY - 1, 8, rows), f32),
            dma((NY,)), dma((NY,)),
            dma((5,)), dma((5,)),
            dma((2, n)), dma((2, n)),
            dma((n,)), dma((n,)),
            dma((2, n)), dma((2, n)),
            dma((NY,)), dma((NY,)),
            dma((NY,)), dma((NY,)),
        ],
        compiler_params=pltpu.CompilerParams(
            collective_id=0, has_side_effects=True, vmem_limit_bytes=48 * 2**20),
    )(queries, keys, values, req_lengths)


def solution(mesh):
    placed = (P("seq", "head"), P(("seq", "head"), None), P(("seq", "head"), None), P())
    return jax.shard_map(
        body, mesh=mesh, in_specs=placed, out_specs=P("seq", "head"), check_vma=False
    )
```

```python
import functools
import math

import jax
import jax.numpy as jnp
from jax import lax
from jax.experimental import pallas as pl
from jax.experimental.pallas import tpu as pltpu
from jax.sharding import PartitionSpec as P

HD = 128
PAGE = 128
NX, NY, NZ = 4, 4, 16
REQS = 16
SCALE = math.log2(math.e) / math.sqrt(HD)
LOW = -1e15
BIG = 1e30
NT = (((1,), (1,)), ((), ()))
NN = (((1,), (0,)), ((), ()))
MESH = pl.DeviceIdType.MESH


def dot(a, b, dims):
    return lax.dot_general(a, b, dims, preferred_element_type=jnp.float32)


def kernel(q_ref, k_ref, v_ref, len_ref, o_ref,
           qbuf, kv, acc, mrow, starts, obuf, lbuf, osend, lsend,
           in_sem, q_ss, q_rs, own_ss, own_rs, far_ss, near_ss, z_rs, x_ss, x_rs, d_ss, d_rs,
           o_ss, o_rs, l_ss, l_rs):
    rows = qbuf.shape[1]
    seq = lax.axis_index("seq")
    head = lax.axis_index("head")
    x, z = seq // NZ, seq % NZ
    y, c = head // 2, head % 2

    def at(dx, dy, dz, core):
        xx = (x + dx + NX) % NX
        yy = (y + dy) % NY
        zz = (z + dz + NZ) % NZ
        return (xx * NZ + zz, yy * 2 + core)

    def flip(u, v):
        return (u % 2 + v % 2) % 2 + 2 * ((u // 2 + v // 2) % 2)

    def plane(a, j):
        return 4 * flip(z // 4, a) + flip(z % 4, j)

    def along(a, j):
        return (x * NZ + plane(a, j), y * 2 + c)

    late = z >= NZ // 2
    sibling = at(0, 0, 0, 1 - c)
    barrier = pltpu.get_barrier_semaphore()
    partners = [sibling] + [along(1, 0), along(0, 1), along(0, 2), along(0, 3)]
    partners += [at(dx, 0, 0, c) for dx in (1, -1, 2)]
    partners += [at(0, dy, 0, c) for dy in (1, 2, 3)]
    for partner in partners:
        pl.semaphore_signal(barrier, inc=1, device_id=partner, device_id_type=MESH)

    @pl.when(jnp.logical_not(late))
    def _():
        for a in (2, 3):
            pl.semaphore_signal(barrier, inc=1, device_id=along(a, 0), device_id_type=MESH)

    def slot(dx, zz):
        return dx * NZ + zz

    inputs = [
        pltpu.make_async_copy(k_ref, kv.at[slot(0, z), c, 0], in_sem.at[0]),
        pltpu.make_async_copy(v_ref, kv.at[slot(0, z), c, 1], in_sem.at[1]),
        pltpu.make_async_copy(q_ref, qbuf.at[0], in_sem.at[2]),
    ]
    for copy in inputs:
        copy.start()

    acc[...] = jnp.zeros_like(acc)
    mrow[...] = jnp.full_like(mrow, LOW)
    row_page = seq * (rows // PAGE) + lax.broadcasted_iota(jnp.int32, (1, rows), 1) // PAGE
    start = jnp.int32(0)
    found = jnp.zeros((1, rows), jnp.int32)
    for r in range(REQS):
        found = jnp.maximum(found, jnp.where(row_page >= start, start, 0))
        start = start + len_ref[r]
    starts[...] = found

    @pl.when(x < 2)
    def _():
        kv[2 * NZ:] = jnp.zeros((NZ,) + kv.shape[1:], kv.dtype)

    for copy in inputs:
        copy.wait()
    pl.semaphore_wait(barrier, len(partners) + 2 * (z // (NZ // 2)))

    def remote(src, dst, ssem, rsem, to):
        return pltpu.make_async_remote_copy(
            src_ref=src, dst_ref=dst, send_sem=ssem, recv_sem=rsem, device_id=to, device_id_type=MESH)

    def q_copy(j):
        return remote(qbuf.at[0], qbuf.at[j], q_ss.at[j], q_rs.at[j], at(0, NY - j, 0, c))

    def half(dx, zz, core):
        return kv.at[slot(dx, zz), core]

    def own_copy():
        return remote(half(0, z, c), half(0, z, c), own_ss.at[0], own_rs.at[0], sibling)

    def far_copy(a):
        return remote(half(0, z, c), half(0, z, c), far_ss.at[a - 1], z_rs.at[z], along(a, 0))

    def near_copy(j, zz):
        return remote(half(0, zz, c), half(0, zz, c), near_ss.at[j - 1, zz // 4], z_rs.at[zz], along(0, j))

    def z_wait(zz):
        remote(half(0, zz, c), half(0, zz, c), far_ss.at[0], z_rs.at[zz], sibling).wait_recv()

    def x_copy(dx, zz):
        return remote(half(0, zz, c), half(dx, zz, c), x_ss.at[dx - 1, zz], x_rs.at[dx - 1, zz], at(dx, 0, 0, c))

    def x_wait(dx, zz):
        remote(half(dx, zz, c), half(dx, zz, c), x_ss.at[dx - 1, zz], x_rs.at[dx - 1, zz], sibling).wait_recv()

    def far(zz):
        return jnp.where(zz < z, 0, 2)

    def d_copy(part, zz, core):
        dx = 1 if part else far(zz)
        return remote(half(dx, zz, core), half(dx, zz, core), d_ss.at[part, zz], d_rs.at[part, zz], sibling)

    def pair(n):
        a, j = 2 * (n // 4), n % 4
        return plane(a, j), plane(a + 1, j)

    def share(zz):
        x_copy(1, zz).start()

        @pl.when((zz >= z) & (x < 2))
        def _():
            x_copy(2, zz).start()

        @pl.when(zz < z)
        def _():
            d_copy(0, zz, c).start()

    def spread(zz):
        for j in (1, 2, 3):
            near_copy(j, zz).start()

    def own_row(n):
        for zz in pair(n):
            z_wait(zz)
            share(zz)

    def other_half():
        for a in (2, 3):
            zz = plane(a, 0)
            z_wait(zz)
            spread(zz)

            @pl.when(jnp.logical_not(late))
            def _():
                far_copy(a).start()
            share(zz)

    def other_rows(n):
        for zz in pair(n):
            x_wait(1, zz)
            d_copy(1, zz, c).start()

            @pl.when((zz >= z) & (x >= 2))
            def _():
                x_wait(2, zz)
                d_copy(0, zz, c).start()

    def arrived(n):
        for zz in pair(n):
            d_copy(1, zz, 1 - c).wait_recv()

            @pl.when((zz < z) | (x >= 2))
            def _():
                d_copy(0, zz, 1 - c).wait_recv()

    def page_of(dx, zz):
        return ((x - dx) * NZ + zz) * (rows // PAGE) + y

    def chunk(pages, heads, diagonal=None, after=None):
        slots = [slot(dx, zz) for dx, zz in pages]
        ks = jnp.concatenate([kv[s, i, 0] for s in slots for i in (0, 1)], axis=0)
        vs = jnp.concatenate([kv[s, i, 1] for s in slots for i in (0, 1)], axis=0)
        vt = jnp.concatenate([vs.T, jnp.ones((16, vs.shape[0]), jnp.bfloat16)], axis=0)
        first = starts[...]
        bias = [jnp.where(first <= page_of(dx, zz), 0.0, -BIG) for dx, zz in pages]
        if diagonal is not None:
            key = y * PAGE + lax.broadcasted_iota(jnp.int32, (PAGE, rows), 0)
            row = lax.broadcasted_iota(jnp.int32, (PAGE, rows), 1)
            causal = key <= row
        scores = [dot(ks, qbuf[h], NT) for h in heads]
        for h, st in zip(heads, scores):
            old = mrow[h]
            new = old
            parts = []
            for n in range(len(pages)):
                part = st[n * PAGE:(n + 1) * PAGE] * SCALE
                if n == diagonal:
                    part = jnp.where(causal, part, -BIG)
                parts.append(part)
                new = jnp.maximum(new, jnp.max(part, axis=0, keepdims=True) + bias[n])
            terms = [jnp.exp2(parts[n] - (new - bias[n])) for n in range(len(pages))]
            factor = jnp.exp2(old - new)
            mrow[h] = new
            update = dot(vt, jnp.concatenate(terms, axis=0).astype(jnp.bfloat16), NN)
            acc[h] = acc[h] * factor + update
            if after is not None:
                after(h)

    def pages(n):
        a, b = pair(n)
        return [(far(a), a), (far(b), b), (1, a), (1, b)]

    def finish(h):
        total = jnp.maximum(acc[h, HD:HD + 1, :], 1e-30)
        part = acc[h, :HD, :] / total
        level = mrow[h] + jnp.log2(total)
        return part, level

    def o_copy(j):
        return remote(osend.at[j - 1], obuf.at[j - 1], o_ss.at[j], o_rs.at[j], at(0, j, 0, c))

    def l_copy(j):
        return remote(lsend.at[j - 1], lbuf.at[j - 1], l_ss.at[j], l_rs.at[j], at(0, j, 0, c))

    def give(h):
        if h > 0:
            part, level = finish(h)
            osend[h - 1] = part.astype(jnp.bfloat16)
            lsend[h - 1] = jnp.broadcast_to(level, lsend.shape[1:])
            o_copy(h).start()
            l_copy(h).start()

    @pl.when(late)
    def _():
        far_copy(2).start()
        far_copy(3).start()
    far_copy(1).start()
    own_copy().start()
    spread(z)
    share(z)
    for j in (1, 3, 2):
        q_copy(j).start()
    fourth = plane(1, 0)
    z_wait(fourth)
    spread(fourth)
    share(fourth)
    own_row(1)
    remote(half(0, z, 1 - c), half(0, z, 1 - c), own_ss.at[0], own_rs.at[0], sibling).wait_recv()
    for j in (1, 3, 2):
        q_copy(j).wait_recv()
    everyone = [2, 1, 3, 0]
    chunk([(0, z)], everyone, 0)

    def turn(n, _):
        @pl.when((n < 8) & (n != 4))
        def _():
            own_row(n)

        @pl.when(n == 4)
        def _():
            other_half()

        @pl.when((n >= 3) & (n < 8 + 3))
        def _():
            other_rows(n - 3)

        @pl.when(n >= 4)
        def _():
            arrived(n - 4)
            chunk(pages(n - 4), everyone)
        return 0

    lax.fori_loop(2, 7 + 4, turn, 0)
    arrived(7)
    chunk(pages(7), everyone, after=give)

    part, level = finish(0)
    for j in (1, 2, 3):
        o_copy(j).wait_recv()
        l_copy(j).wait_recv()
    levels = [level] + [lbuf[j, 0:1, :] for j in range(3)]
    top = functools.reduce(jnp.maximum, levels)
    shares = [jnp.exp2(level - top) for level in levels]
    total = functools.reduce(jnp.add, shares)
    mixed = part * (shares[0] / total)
    for j in range(3):
        mixed = mixed + obuf[j].astype(jnp.float32) * (shares[j + 1] / total)
    o_ref[...] = mixed.T.astype(o_ref.dtype)

    own_copy().wait_send()
    for a in (1, 2, 3):
        far_copy(a).wait_send()
    for j in (1, 2, 3):
        q_copy(j).wait_send()
        o_copy(j).wait_send()
        l_copy(j).wait_send()

    def drain_near(a, _):
        for j in (1, 2, 3):
            near_copy(j, a * 4 + z % 4).wait_send()
        return 0

    def drain(zz, _):
        x_copy(1, zz).wait_send()
        d_copy(1, zz, c).wait_send()

        @pl.when((zz >= z) & (x < 2))
        def _():
            x_copy(2, zz).wait_send()

        @pl.when((zz < z) | (x >= 2))
        def _():
            d_copy(0, zz, c).wait_send()
        return 0

    lax.fori_loop(0, 4, drain_near, 0)
    lax.fori_loop(0, NZ, drain, 0)


def body(queries, keys, values, req_lengths):
    rows = queries.shape[0]
    bf, f32, dma = jnp.bfloat16, jnp.float32, pltpu.SemaphoreType.DMA
    return pl.pallas_call(
        kernel,
        out_shape=jax.ShapeDtypeStruct((rows, HD), bf),
        in_specs=[pl.BlockSpec(memory_space=pl.ANY)] * 3 + [pl.BlockSpec(memory_space=pltpu.SMEM)],
        out_specs=pl.BlockSpec(memory_space=pltpu.VMEM),
        scratch_shapes=[
            pltpu.VMEM((NY, rows, HD), bf),
            pltpu.VMEM((3 * NZ, 2, 2, PAGE // 2, HD), bf),
            pltpu.VMEM((NY, HD + 16, rows), f32),
            pltpu.VMEM((NY, 1, rows), f32),
            pltpu.VMEM((1, rows), jnp.int32),
            pltpu.VMEM((NY - 1, HD, rows), bf),
            pltpu.VMEM((NY - 1, 8, rows), f32),
            pltpu.VMEM((NY - 1, HD, rows), bf),
            pltpu.VMEM((NY - 1, 8, rows), f32),
            dma((3,)),
            dma((NY,)), dma((NY,)),
            dma((1,)), dma((1,)),
            dma((3,)), dma((3, 4)), dma((NZ,)),
            dma((2, NZ)), dma((2, NZ)),
            dma((2, NZ)), dma((2, NZ)),
            dma((NY,)), dma((NY,)),
            dma((NY,)), dma((NY,)),
        ],
        compiler_params=pltpu.CompilerParams(
            collective_id=0, has_side_effects=True, vmem_limit_bytes=60 * 2**20),
    )(queries, keys, values, req_lengths)


def solution(mesh):
    placed = (P("seq", "head"), P(("seq", "head"), None), P(("seq", "head"), None), P())
    return jax.shard_map(
        body, mesh=mesh, in_specs=placed, out_specs=P("seq", "head"), check_vma=False
    )
```

```python
import functools
import math

import jax
import jax.numpy as jnp
from jax import lax
from jax.experimental import pallas as pl
from jax.experimental.pallas import tpu as pltpu
from jax.sharding import PartitionSpec as P

HD = 128
PAGE = 128
NX, NY, NZ = 4, 4, 16
REQS = 16
SCALE = math.log2(math.e) / math.sqrt(HD)
LOW = -1e15
BIG = 1e30
NT = (((1,), (1,)), ((), ()))
NN = (((1,), (0,)), ((), ()))
MESH = pl.DeviceIdType.MESH


def dot(a, b, dims):
    return lax.dot_general(a, b, dims, preferred_element_type=jnp.float32)


def kernel(q_ref, k_ref, v_ref, len_ref, o_ref,
           qbuf, kv, acc, mrow, starts, obuf, lbuf, osend, lsend,
           in_sem, hello, q_ss, q_rs, own_ss, own_rs, far_ss, near_ss, z_rs, x_ss, x_rs, d_ss, d_rs,
           o_ss, o_rs, l_ss, l_rs):
    rows = qbuf.shape[1]
    seq = lax.axis_index("seq")
    head = lax.axis_index("head")
    x, z = seq // NZ, seq % NZ
    y, c = head // 2, head % 2

    def at(dx, dy, dz, core):
        xx = (x + dx + NX) % NX
        yy = (y + dy) % NY
        zz = (z + dz + NZ) % NZ
        return (xx * NZ + zz, yy * 2 + core)

    def flip(u, v):
        return (u % 2 + v % 2) % 2 + 2 * ((u // 2 + v // 2) % 2)

    def plane(a, j):
        return 4 * flip(z // 4, a) + flip(z % 4, j)

    def along(a, j):
        return (x * NZ + plane(a, j), y * 2 + c)

    late = z >= NZ // 2
    sibling = at(0, 0, 0, 1 - c)
    barrier = pltpu.get_barrier_semaphore()
    partners = [sibling] + [along(1, 0), along(0, 1), along(0, 2), along(0, 3)]
    partners += [at(dx, 0, 0, c) for dx in (1, -1, 2)]
    partners += [at(0, dy, 0, c) for dy in (1, 2, 3)]
    for partner in partners:
        pl.semaphore_signal(barrier, inc=1, device_id=partner, device_id_type=MESH)

    @pl.when(jnp.logical_not(late))
    def _():
        for a in (2, 3):
            pl.semaphore_signal(barrier, inc=1, device_id=along(a, 0), device_id_type=MESH)

    def slot(dx, zz):
        return dx * NZ + zz

    inputs = [
        pltpu.make_async_copy(k_ref, kv.at[slot(0, z), c, 0], in_sem.at[0]),
        pltpu.make_async_copy(v_ref, kv.at[slot(0, z), c, 1], in_sem.at[1]),
        pltpu.make_async_copy(q_ref, qbuf.at[0], in_sem.at[2]),
    ]
    for copy in inputs:
        copy.start()

    acc[...] = jnp.zeros_like(acc)
    mrow[...] = jnp.full_like(mrow, LOW)
    row_page = seq * (rows // PAGE) + lax.broadcasted_iota(jnp.int32, (1, rows), 1) // PAGE
    start = jnp.int32(0)
    found = jnp.zeros((1, rows), jnp.int32)
    for r in range(REQS):
        found = jnp.maximum(found, jnp.where(row_page >= start, start, 0))
        start = start + len_ref[r]
    starts[...] = found

    @pl.when(x == 0)
    def _():
        kv[NZ:2 * NZ] = jnp.zeros((NZ,) + kv.shape[1:], kv.dtype)

    @pl.when(x < 2)
    def _():
        kv[2 * NZ:] = jnp.zeros((NZ,) + kv.shape[1:], kv.dtype)

    for copy in inputs:
        copy.wait()
    pl.semaphore_wait(barrier, len(partners) + 2 * (z // (NZ // 2)))

    def remote(src, dst, ssem, rsem, to):
        return pltpu.make_async_remote_copy(
            src_ref=src, dst_ref=dst, send_sem=ssem, recv_sem=rsem, device_id=to, device_id_type=MESH)

    def q_copy(j):
        return remote(qbuf.at[0], qbuf.at[j], q_ss.at[j], q_rs.at[j], at(0, NY - j, 0, c))

    def half(dx, zz, core):
        return kv.at[slot(dx, zz), core]

    def own_copy():
        return remote(half(0, z, c), half(0, z, c), own_ss.at[0], own_rs.at[0], sibling)

    def far_copy(a):
        return remote(half(0, z, c), half(0, z, c), far_ss.at[a - 1], z_rs.at[z], along(a, 0))

    def near_copy(j, zz):
        return remote(half(0, zz, c), half(0, zz, c), near_ss.at[j - 1, zz // 4], z_rs.at[zz], along(0, j))

    def z_wait(zz):
        remote(half(0, zz, c), half(0, zz, c), far_ss.at[0], z_rs.at[zz], sibling).wait_recv()

    def x_copy(dx, zz):
        return remote(half(0, zz, c), half(dx, zz, c), x_ss.at[dx - 1, zz], x_rs.at[dx - 1, zz], at(dx, 0, 0, c))

    def x_wait(dx, zz):
        remote(half(dx, zz, c), half(dx, zz, c), x_ss.at[dx - 1, zz], x_rs.at[dx - 1, zz], sibling).wait_recv()

    def far(zz):
        return jnp.where(zz < z, 0, 2)

    def d_copy(part, zz, core):
        dx = 1 if part else far(zz)
        return remote(half(dx, zz, core), half(dx, zz, core), d_ss.at[part, zz], d_rs.at[part, zz], sibling)

    def pair(n):
        a, j = 2 * (n // 4), n % 4
        return plane(a, j), plane(a + 1, j)

    def share(zz):
        @pl.when(x < NX - 1)
        def _():
            x_copy(1, zz).start()

        @pl.when((zz >= z) & (x < 2))
        def _():
            x_copy(2, zz).start()

        @pl.when(zz < z)
        def _():
            d_copy(0, zz, c).start()

    def spread(zz):
        for j in (1, 2, 3):
            near_copy(j, zz).start()

    def own_row(n):
        for zz in pair(n):
            z_wait(zz)
            share(zz)

    def other_half():
        @pl.when(jnp.logical_not(late))
        def _():
            for a in (2, 3):
                pl.semaphore_wait(hello.at[a - 2], 1)
                far_copy(a).start()

        for a in (2, 3):
            zz = plane(a, 0)
            z_wait(zz)
            spread(zz)
            share(zz)

    def other_rows(n):
        for zz in pair(n):
            @pl.when(x > 0)
            def _():
                x_wait(1, zz)
                d_copy(1, zz, c).start()

            @pl.when((zz >= z) & (x >= 2))
            def _():
                x_wait(2, zz)
                d_copy(0, zz, c).start()

    def arrived(n):
        for zz in pair(n):
            @pl.when(x > 0)
            def _():
                d_copy(1, zz, 1 - c).wait_recv()

            @pl.when((zz < z) | (x >= 2))
            def _():
                d_copy(0, zz, 1 - c).wait_recv()

    def page_of(dx, zz):
        return ((x - dx) * NZ + zz) * (rows // PAGE) + y

    def chunk(pages, heads, diagonal=None, after=None):
        slots = [slot(dx, zz) for dx, zz in pages]
        ks = jnp.concatenate([kv[s, i, 0] for s in slots for i in (0, 1)], axis=0)
        vs = jnp.concatenate([kv[s, i, 1] for s in slots for i in (0, 1)], axis=0)
        vt = jnp.concatenate([vs.T, jnp.ones((16, vs.shape[0]), jnp.bfloat16)], axis=0)
        first = starts[...]
        bias = [jnp.where(first <= page_of(dx, zz), 0.0, -BIG) for dx, zz in pages]
        if diagonal is not None:
            key = y * PAGE + lax.broadcasted_iota(jnp.int32, (PAGE, rows), 0)
            row = lax.broadcasted_iota(jnp.int32, (PAGE, rows), 1)
            causal = key <= row
        scores = [dot(ks, qbuf[h], NT) for h in heads]
        for h, st in zip(heads, scores):
            old = mrow[h]
            new = old
            parts = []
            for n in range(len(pages)):
                part = st[n * PAGE:(n + 1) * PAGE] * SCALE
                if n == diagonal:
                    part = jnp.where(causal, part, -BIG)
                parts.append(part)
                new = jnp.maximum(new, jnp.max(part, axis=0, keepdims=True) + bias[n])
            terms = [jnp.exp2(parts[n] - (new - bias[n])) for n in range(len(pages))]
            factor = jnp.exp2(old - new)
            mrow[h] = new
            update = dot(vt, jnp.concatenate(terms, axis=0).astype(jnp.bfloat16), NN)
            acc[h] = acc[h] * factor + update
            if after is not None:
                after(h)

    def pages(n):
        a, b = pair(n)
        return [(far(a), a), (far(b), b), (1, a), (1, b)]

    def finish(h):
        total = jnp.maximum(acc[h, HD:HD + 1, :], 1e-30)
        part = acc[h, :HD, :] * (1.0 / total)
        level = mrow[h] + jnp.log2(total)
        return part, level

    def o_copy(j):
        return remote(osend.at[j - 1], obuf.at[j - 1], o_ss.at[j], o_rs.at[j], at(0, j, 0, c))

    def l_copy(j):
        return remote(lsend.at[j - 1], lbuf.at[j - 1], l_ss.at[j], l_rs.at[j], at(0, j, 0, c))

    def give(h):
        if h > 0:
            part, level = finish(h)
            osend[h - 1] = part.astype(jnp.bfloat16)
            lsend[h - 1] = jnp.broadcast_to(level, lsend.shape[1:])
            o_copy(h).start()
            l_copy(h).start()

    @pl.when(late)
    def _():
        for a in (2, 3):
            pl.semaphore_signal(hello.at[a - 2], inc=1, device_id=along(a, 0), device_id_type=MESH)
        far_copy(2).start()
        far_copy(3).start()
    far_copy(1).start()
    own_copy().start()
    spread(z)
    share(z)
    for j in (1, 3, 2):
        q_copy(j).start()
    fourth = plane(1, 0)
    z_wait(fourth)
    spread(fourth)
    share(fourth)
    own_row(1)
    given = [2, 1, 3]

    def begin():
        remote(half(0, z, 1 - c), half(0, z, 1 - c), own_ss.at[0], own_rs.at[0], sibling).wait_recv()
        for j in (1, 3, 2):
            q_copy(j).wait_recv()
        chunk([(0, z)], given, 0)

    def turn(n, _):
        @pl.when((n < 8) & (n != 4))
        def _():
            own_row(n)

        @pl.when(n == 4)
        def _():
            other_half()

        @pl.when((n >= 3) & (n < 8 + 3))
        def _():
            other_rows(n - 3)

        @pl.when(n == 4)
        def _():
            begin()

        @pl.when(n >= 4)
        def _():
            arrived(n - 4)
            chunk(pages(n - 4), given)
        return 0

    lax.fori_loop(2, 7 + 4, turn, 0)
    arrived(7)
    chunk(pages(7), given, after=give)
    chunk([(0, z)], [0], 0)

    def own_head(n, _):
        chunk(pages(n), [0])
        return 0

    lax.fori_loop(0, 8, own_head, 0)
    part, level = finish(0)
    for j in (1, 2, 3):
        o_copy(j).wait_recv()
        l_copy(j).wait_recv()
    levels = [level] + [lbuf[j, 0:1, :] for j in range(3)]
    top = functools.reduce(jnp.maximum, levels)
    shares = [jnp.exp2(level - top) for level in levels]
    total = functools.reduce(jnp.add, shares)
    mixed = part * (shares[0] / total)
    for j in range(3):
        mixed = mixed + obuf[j].astype(jnp.float32) * (shares[j + 1] / total)
    o_ref[...] = mixed.T.astype(o_ref.dtype)

    own_copy().wait_send()
    for a in (1, 2, 3):
        far_copy(a).wait_send()
    for j in (1, 2, 3):
        q_copy(j).wait_send()
        o_copy(j).wait_send()
        l_copy(j).wait_send()

    def drain_near(a, _):
        for j in (1, 2, 3):
            near_copy(j, a * 4 + z % 4).wait_send()
        return 0

    def drain(zz, _):
        @pl.when(x < NX - 1)
        def _():
            x_copy(1, zz).wait_send()

        @pl.when(x > 0)
        def _():
            d_copy(1, zz, c).wait_send()

        @pl.when((zz >= z) & (x < 2))
        def _():
            x_copy(2, zz).wait_send()

        @pl.when((zz < z) | (x >= 2))
        def _():
            d_copy(0, zz, c).wait_send()
        return 0

    lax.fori_loop(0, 4, drain_near, 0)
    lax.fori_loop(0, NZ, drain, 0)


def body(queries, keys, values, req_lengths):
    rows = queries.shape[0]
    bf, f32, dma = jnp.bfloat16, jnp.float32, pltpu.SemaphoreType.DMA
    return pl.pallas_call(
        kernel,
        out_shape=jax.ShapeDtypeStruct((rows, HD), bf),
        in_specs=[pl.BlockSpec(memory_space=pl.ANY)] * 3 + [pl.BlockSpec(memory_space=pltpu.SMEM)],
        out_specs=pl.BlockSpec(memory_space=pltpu.VMEM),
        scratch_shapes=[
            pltpu.VMEM((NY, rows, HD), bf),
            pltpu.VMEM((3 * NZ, 2, 2, PAGE // 2, HD), bf),
            pltpu.VMEM((NY, HD + 16, rows), f32),
            pltpu.VMEM((NY, 1, rows), f32),
            pltpu.VMEM((1, rows), jnp.int32),
            pltpu.VMEM((NY - 1, HD, rows), bf),
            pltpu.VMEM((NY - 1, 8, rows), f32),
            pltpu.VMEM((NY - 1, HD, rows), bf),
            pltpu.VMEM((NY - 1, 8, rows), f32),
            dma((3,)), pltpu.SemaphoreType.REGULAR((6,)),
            dma((NY,)), dma((NY,)),
            dma((1,)), dma((1,)),
            dma((3,)), dma((3, 4)), dma((NZ,)),
            dma((2, NZ)), dma((2, NZ)),
            dma((2, NZ)), dma((2, NZ)),
            dma((NY,)), dma((NY,)),
            dma((NY,)), dma((NY,)),
        ],
        compiler_params=pltpu.CompilerParams(
            collective_id=0, has_side_effects=True, vmem_limit_bytes=60 * 2**20),
    )(queries, keys, values, req_lengths)


def solution(mesh):
    placed = (P("seq", "head"), P(("seq", "head"), None), P(("seq", "head"), None), P())
    return jax.shard_map(
        body, mesh=mesh, in_specs=placed, out_specs=P("seq", "head"), check_vma=False
    )
```

```python
import functools
import math

import jax
import jax.numpy as jnp
from jax import lax
from jax.experimental import pallas as pl
from jax.experimental.pallas import tpu as pltpu
from jax.sharding import PartitionSpec as P

HD = 128
PAGE = 128
NX, NY, NZ = 4, 4, 16
REQS = 16
SCALE = math.log2(math.e) / math.sqrt(HD)
LOW = -1e15
BIG = 1e30
NT = (((1,), (1,)), ((), ()))
NN = (((1,), (0,)), ((), ()))
MESH = pl.DeviceIdType.MESH


def dot(a, b, dims):
    return lax.dot_general(a, b, dims, preferred_element_type=jnp.float32)


def kernel(q_ref, k_ref, v_ref, len_ref, o_ref,
           qbuf, kv, acc, mrow, starts, obuf, lbuf, osend, lsend,
           in_sem, hello, q_ss, q_rs, own_ss, own_rs, far_ss, near_ss, z_rs, x_ss, x_rs, d_ss, d_rs,
           o_ss, o_rs, l_ss, l_rs):
    rows = qbuf.shape[1]
    seq = lax.axis_index("seq")
    head = lax.axis_index("head")
    x, z = seq // NZ, seq % NZ
    y, c = head // 2, head % 2

    def at(dx, dy, dz, core):
        xx = (x + dx + NX) % NX
        yy = (y + dy) % NY
        zz = (z + dz + NZ) % NZ
        return (xx * NZ + zz, yy * 2 + core)

    def flip(u, v):
        return (u % 2 + v % 2) % 2 + 2 * ((u // 2 + v // 2) % 2)

    def plane(a, j):
        return 4 * flip(z // 4, a) + flip(z % 4, j)

    def along(a, j):
        return (x * NZ + plane(a, j), y * 2 + c)

    late = z >= NZ // 2
    sibling = at(0, 0, 0, 1 - c)
    barrier = pltpu.get_barrier_semaphore()
    partners = [sibling] + [along(1, 0), along(0, 1), along(0, 2), along(0, 3)]
    partners += [at(dx, 0, 0, c) for dx in (1, -1, 2)]
    partners += [at(0, dy, 0, c) for dy in (1, 2, 3)]
    for partner in partners:
        pl.semaphore_signal(barrier, inc=1, device_id=partner, device_id_type=MESH)

    @pl.when(jnp.logical_not(late))
    def _():
        for a in (2, 3):
            pl.semaphore_signal(barrier, inc=1, device_id=along(a, 0), device_id_type=MESH)

    def slot(dx, zz):
        return dx * NZ + zz

    inputs = [
        pltpu.make_async_copy(k_ref, kv.at[slot(0, z), c, 0], in_sem.at[0]),
        pltpu.make_async_copy(v_ref, kv.at[slot(0, z), c, 1], in_sem.at[1]),
        pltpu.make_async_copy(q_ref, qbuf.at[0], in_sem.at[2]),
    ]
    for copy in inputs:
        copy.start()

    for copy in inputs:
        copy.wait()
    pl.semaphore_wait(barrier, len(partners) + 2 * (z // (NZ // 2)))

    def remote(src, dst, ssem, rsem, to):
        return pltpu.make_async_remote_copy(
            src_ref=src, dst_ref=dst, send_sem=ssem, recv_sem=rsem, device_id=to, device_id_type=MESH)

    def q_copy(j):
        return remote(qbuf.at[0], qbuf.at[j], q_ss.at[j], q_rs.at[j], at(0, NY - j, 0, c))

    def half(dx, zz, core):
        return kv.at[slot(dx, zz), core]

    def own_copy():
        return remote(half(0, z, c), half(0, z, c), own_ss.at[0], own_rs.at[0], sibling)

    def far_copy(a):
        return remote(half(0, z, c), half(0, z, c), far_ss.at[a - 1], z_rs.at[z], along(a, 0))

    def near_copy(j, zz):
        return remote(half(0, zz, c), half(0, zz, c), near_ss.at[j - 1, zz // 4], z_rs.at[zz], along(0, j))

    def z_wait(zz):
        remote(half(0, zz, c), half(0, zz, c), far_ss.at[0], z_rs.at[zz], sibling).wait_recv()

    def x_copy(dx, zz):
        return remote(half(0, zz, c), half(dx, zz, c), x_ss.at[dx - 1, zz], x_rs.at[dx - 1, zz], at(dx, 0, 0, c))

    def x_wait(dx, zz):
        remote(half(dx, zz, c), half(dx, zz, c), x_ss.at[dx - 1, zz], x_rs.at[dx - 1, zz], sibling).wait_recv()

    def far(zz):
        return jnp.where(zz < z, 0, 2)

    def d_copy(part, zz, core):
        dx = 1 if part else far(zz)
        return remote(half(dx, zz, core), half(dx, zz, core), d_ss.at[part, zz], d_rs.at[part, zz], sibling)

    def pair(n):
        a, j = 2 * (n // 4), n % 4
        return plane(a, j), plane(a + 1, j)

    def share(zz):
        @pl.when(x < NX - 1)
        def _():
            x_copy(1, zz).start()

        @pl.when((zz >= z) & (x < 2))
        def _():
            x_copy(2, zz).start()

        @pl.when(zz < z)
        def _():
            d_copy(0, zz, c).start()

    def spread(zz):
        for j in (1, 2, 3):
            near_copy(j, zz).start()

    def own_row(n):
        for zz in pair(n):
            z_wait(zz)
            share(zz)

    def other_half():
        @pl.when(jnp.logical_not(late))
        def _():
            for a in (2, 3):
                pl.semaphore_wait(hello.at[a - 2], 1)
                far_copy(a).start()

        for a in (2, 3):
            zz = plane(a, 0)
            z_wait(zz)
            spread(zz)
            share(zz)

    def other_rows(n):
        for zz in pair(n):
            @pl.when(x > 0)
            def _():
                x_wait(1, zz)
                d_copy(1, zz, c).start()

            @pl.when((zz >= z) & (x >= 2))
            def _():
                x_wait(2, zz)
                d_copy(0, zz, c).start()

    def arrived(n):
        for zz in pair(n):
            @pl.when(x > 0)
            def _():
                d_copy(1, zz, 1 - c).wait_recv()

            @pl.when((zz < z) | (x >= 2))
            def _():
                d_copy(0, zz, 1 - c).wait_recv()

    def page_of(dx, zz):
        return ((x - dx) * NZ + zz) * (rows // PAGE) + y

    def chunk(pages, heads, diagonal=None, after=None):
        slots = [slot(dx, zz) for dx, zz in pages]
        ks = jnp.concatenate([kv[s, i, 0] for s in slots for i in (0, 1)], axis=0)
        vs = jnp.concatenate([kv[s, i, 1] for s in slots for i in (0, 1)], axis=0)
        vt = jnp.concatenate([vs.T, jnp.ones((16, vs.shape[0]), jnp.bfloat16)], axis=0)
        first = starts[...]
        bias = [jnp.where(first <= page_of(dx, zz), 0.0, -BIG) for dx, zz in pages]
        if diagonal is not None:
            key = y * PAGE + lax.broadcasted_iota(jnp.int32, (PAGE, rows), 0)
            row = lax.broadcasted_iota(jnp.int32, (PAGE, rows), 1)
            causal = key <= row
        scores = [dot(ks, qbuf[h], NT) for h in heads]
        for h, st in zip(heads, scores):
            old = mrow[h]
            new = old
            parts = []
            for n in range(len(pages)):
                part = st[n * PAGE:(n + 1) * PAGE] * SCALE
                if n == diagonal:
                    part = jnp.where(causal, part, -BIG)
                parts.append(part)
                new = jnp.maximum(new, jnp.max(part, axis=0, keepdims=True) + bias[n])
            terms = [jnp.exp2(parts[n] - (new - bias[n])) for n in range(len(pages))]
            factor = jnp.exp2(old - new)
            mrow[h] = new
            update = dot(vt, jnp.concatenate(terms, axis=0).astype(jnp.bfloat16), NN)
            acc[h] = acc[h] * factor + update
            if after is not None:
                after(h)

    def pages(n):
        a, b = pair(n)
        return [(far(a), a), (far(b), b), (1, a), (1, b)]

    def finish(h):
        total = jnp.maximum(acc[h, HD:HD + 1, :], 1e-30)
        part = acc[h, :HD, :] * (1.0 / total)
        level = mrow[h] + jnp.log2(total)
        return part, level

    def o_copy(j):
        return remote(osend.at[j - 1], obuf.at[j - 1], o_ss.at[j], o_rs.at[j], at(0, j, 0, c))

    def l_copy(j):
        return remote(lsend.at[j - 1], lbuf.at[j - 1], l_ss.at[j], l_rs.at[j], at(0, j, 0, c))

    def give(h):
        if h > 0:
            part, level = finish(h)
            osend[h - 1] = part.astype(jnp.bfloat16)
            lsend[h - 1] = level
            o_copy(h).start()
            l_copy(h).start()

    @pl.when(late)
    def _():
        for a in (2, 3):
            pl.semaphore_signal(hello.at[a - 2], inc=1, device_id=along(a, 0), device_id_type=MESH)
        far_copy(2).start()
        far_copy(3).start()
    far_copy(1).start()
    own_copy().start()
    spread(z)
    share(z)
    for j in (1, 3, 2):
        q_copy(j).start()
    acc[...] = jnp.zeros_like(acc)
    mrow[...] = jnp.full_like(mrow, LOW)
    row_page = seq * (rows // PAGE) + lax.broadcasted_iota(jnp.int32, (1, rows), 1) // PAGE
    start = jnp.int32(0)
    found = jnp.zeros((1, rows), jnp.int32)
    for r in range(REQS):
        found = jnp.maximum(found, jnp.where(row_page >= start, start, 0))
        start = start + len_ref[r]
    starts[...] = found

    @pl.when(x == 0)
    def _():
        kv[NZ:2 * NZ] = jnp.zeros((NZ,) + kv.shape[1:], kv.dtype)

    @pl.when(x < 2)
    def _():
        kv[2 * NZ:] = jnp.zeros((NZ,) + kv.shape[1:], kv.dtype)

    fourth = plane(1, 0)
    z_wait(fourth)
    spread(fourth)
    share(fourth)
    own_row(1)
    given = [2, 1, 3]

    def begin():
        remote(half(0, z, 1 - c), half(0, z, 1 - c), own_ss.at[0], own_rs.at[0], sibling).wait_recv()
        for j in (1, 3, 2):
            q_copy(j).wait_recv()
        chunk([(0, z)], given, 0)

    def turn(n, _):
        @pl.when((n < 8) & (n != 4))
        def _():
            own_row(n)

        @pl.when(n == 4)
        def _():
            other_half()

        @pl.when((n >= 3) & (n < 8 + 3))
        def _():
            other_rows(n - 3)

        @pl.when(n == 4)
        def _():
            begin()

        @pl.when(n >= 4)
        def _():
            arrived(n - 4)
            chunk(pages(n - 4), given)
        return 0

    lax.fori_loop(2, 7 + 4, turn, 0)
    arrived(7)
    chunk(pages(7), given, after=give)
    chunk([(0, z)], [0], 0)

    def own_head(n, _):
        chunk(pages(n), [0])
        return 0

    lax.fori_loop(0, 8, own_head, 0)
    own_copy().wait_send()
    for a in (1, 2, 3):
        far_copy(a).wait_send()
    for j in (1, 2, 3):
        q_copy(j).wait_send()

    def drain_near(a, _):
        for j in (1, 2, 3):
            near_copy(j, a * 4 + z % 4).wait_send()
        return 0

    def drain(zz, _):
        @pl.when(x < NX - 1)
        def _():
            x_copy(1, zz).wait_send()

        @pl.when(x > 0)
        def _():
            d_copy(1, zz, c).wait_send()

        @pl.when((zz >= z) & (x < 2))
        def _():
            x_copy(2, zz).wait_send()

        @pl.when((zz < z) | (x >= 2))
        def _():
            d_copy(0, zz, c).wait_send()
        return 0

    lax.fori_loop(0, 4, drain_near, 0)
    lax.fori_loop(0, NZ, drain, 0)

    part, level = finish(0)
    for j in (1, 2, 3):
        o_copy(j).wait_recv()
        l_copy(j).wait_recv()
    levels = [level] + [lbuf[j] for j in range(3)]
    top = functools.reduce(jnp.maximum, levels)
    shares = [jnp.exp2(level - top) for level in levels]
    total = functools.reduce(jnp.add, shares)
    mixed = part * (shares[0] / total)
    for j in range(3):
        mixed = mixed + obuf[j].astype(jnp.float32) * (shares[j + 1] / total)
    o_ref[...] = mixed.T.astype(o_ref.dtype)

    for j in (1, 2, 3):
        o_copy(j).wait_send()
        l_copy(j).wait_send()


def body(queries, keys, values, req_lengths):
    rows = queries.shape[0]
    bf, f32, dma = jnp.bfloat16, jnp.float32, pltpu.SemaphoreType.DMA
    return pl.pallas_call(
        kernel,
        out_shape=jax.ShapeDtypeStruct((rows, HD), bf),
        in_specs=[pl.BlockSpec(memory_space=pl.ANY)] * 3 + [pl.BlockSpec(memory_space=pltpu.SMEM)],
        out_specs=pl.BlockSpec(memory_space=pltpu.VMEM),
        scratch_shapes=[
            pltpu.VMEM((NY, rows, HD), bf),
            pltpu.VMEM((3 * NZ, 2, 2, PAGE // 2, HD), bf),
            pltpu.VMEM((NY, HD + 16, rows), f32),
            pltpu.VMEM((NY, 1, rows), f32),
            pltpu.VMEM((1, rows), jnp.int32),
            pltpu.VMEM((NY - 1, HD, rows), bf),
            pltpu.VMEM((NY - 1, 1, rows), f32),
            pltpu.VMEM((NY - 1, HD, rows), bf),
            pltpu.VMEM((NY - 1, 1, rows), f32),
            dma((3,)), pltpu.SemaphoreType.REGULAR((6,)),
            dma((NY,)), dma((NY,)),
            dma((1,)), dma((1,)),
            dma((3,)), dma((3, 4)), dma((NZ,)),
            dma((2, NZ)), dma((2, NZ)),
            dma((2, NZ)), dma((2, NZ)),
            dma((NY,)), dma((NY,)),
            dma((NY,)), dma((NY,)),
        ],
        compiler_params=pltpu.CompilerParams(
            collective_id=0, has_side_effects=True, vmem_limit_bytes=60 * 2**20),
    )(queries, keys, values, req_lengths)


def solution(mesh):
    placed = (P("seq", "head"), P(("seq", "head"), None), P(("seq", "head"), None), P())
    return jax.shard_map(
        body, mesh=mesh, in_specs=placed, out_specs=P("seq", "head"), check_vma=False
    )
```
